128 devices in a mesh: pool: 2 (over core), dev: 64 (over x, y, z).
Axes of the slice: x: 4, y: 4, z: 4, core: 2. Of those that a mesh axis runs over, the one named last changes fastest.
Arguments:
- queries: bfloat16 [4, 1024, 8, 576], P(None, 'dev'), may hold values from -9 to 9
- new_latent: bfloat16 [4, 1024, 576], P(None, 'dev'), may hold values from -4 to 4
- cache: bfloat16 [1024, 128, 576], P('dev'), may hold values from -4 to 4
- lengths: int32 [1024], P('dev'), may hold values from 4 to 128, as said below
- hidden_in: bfloat16 [4, 1024, 2048], P(None, 'dev'), may hold values from -4 to 4
- norm_gain: float32 [2048], replicated, may hold values from 0.1 to 1.9
- uv_weight: bfloat16 [8, 512, 128], replicated, may hold values from -0.25 to 0.25
- out_weight: bfloat16 [1024, 2048], replicated, may hold values from -0.1875 to 0.1875
- expert_ids: int32 [4, 1024, 6], P(None, 'dev'), may hold values from 0 to 63, as said below
- gate_weight: bfloat16 [4, 1024, 6], P(None, 'dev'), may hold values from 0.049804688 to 0.59765625
- capacity: int32 [64], replicated, may hold values from 2 to 3
- gate_up: bfloat16 [64, 2048, 2816], P('dev'), may hold values from -0.125 to 0.125
- down: bfloat16 [64, 1408, 2048], P('dev'), may hold values from -0.15625 to 0.15625
Outputs:
- output: bfloat16 [4, 1024, 2048], P(None, 'dev', 'pool')
The draws below stay inside these ranges and needn't reach their ends.
Inputs may be any that keep to these rules, and one draw needn't show every extreme that they name: `expert_ids`: each row names 6 different experts; at each step one expert is named by the first 3 requests of every aligned block of 8 requests, and its capacity is 3. `lengths`: every device holds a request of length 128.
All inputs are finite; a program needn't handle non-finite values.
Results may differ from the reference program's by a relative error of at most 0.01.
Values may be sent and summed in bfloat16 or wider, within the bound.
No kernel may reach another device: no remote copies, remote signals or barrier semaphores. Data moves between devices by JAX's collectives and lax.ppermute only.
A program may use at most 128 MiB of HBM per device.

```python
import jax
import jax.numpy as jnp
from jax import lax

D = 2048
HEADS = 8
LAT = 512
ROPE = 64
QKNOPE = 128
VH = 128
FF = 1408
TOPK = 6
CAP = 3
MICRO = 2
STEPS = 4
REQ_DEV = 16
CTX = 128
KV = 576
SPECIALIST_POOL = 64
REQS = 1024


def hot_experts(key):
    return jax.random.randint(jax.random.fold_in(key, 5), (STEPS,), 0, SPECIALIST_POOL)


def draw_queries(key, part):
    shape_all = (STEPS, REQS, HEADS, KV)
    base = jnp.clip(jax.random.normal(jax.random.fold_in(key, 1), shape_all, jnp.float32), -4.0, 4.0)
    return base.astype(jnp.bfloat16)


def draw_cache(key, part):
    shape_all = (REQS, CTX, KV)
    base = jnp.clip(jax.random.normal(jax.random.fold_in(key, 2), shape_all, jnp.float32), -4.0, 4.0)
    return base.astype(jnp.bfloat16)


def draw_lengths(key, part):
    spread_len = jax.random.randint(jax.random.fold_in(key, 41), (REQS,), 4, CTX + 1)
    offset = jax.random.randint(jax.random.fold_in(key, 42), (), 0, REQ_DEV)
    longest_length = jnp.arange(REQS) % REQ_DEV == offset
    return jnp.where(longest_length, CTX, spread_len).astype(jnp.int32)


def draw_expert_ids(key, part):
    frequent_specialists = hot_experts(key)
    noise = jax.random.randint(jax.random.fold_in(key, 21), (STEPS, REQS, SPECIALIST_POOL), 0, 16384)
    favour = jax.random.randint(jax.random.fold_in(key, 22), (SPECIALIST_POOL,), 0, 4) * 8192
    within_tile = jnp.arange(REQS) % (REQ_DEV // MICRO) < CAP
    additive_reward = (jnp.arange(SPECIALIST_POOL)[None, None, :] == frequent_specialists[:, None, None]) & within_tile[None, :, None]
    ranking_whole_number = (noise + favour[None, None, :]) * SPECIALIST_POOL + jnp.arange(SPECIALIST_POOL)[None, None, :]
    ranking_whole_number = ranking_whole_number + additive_reward.astype(jnp.int32) * 2 ** 26
    unused, picked = lax.top_k(ranking_whole_number, TOPK)
    return picked.astype(jnp.int32)


def draw_capacity(key, part):
    frequent_specialists = hot_experts(key)
    base = jax.random.randint(jax.random.fold_in(key, 31), (SPECIALIST_POOL,), 2, CAP + 1)
    is_hot = jnp.any(jnp.arange(SPECIALIST_POOL)[:, None] == frequent_specialists[None, :], axis=1)
    return jnp.where(is_hot, CAP, base).astype(jnp.int32)


def shard_levels(rng, dims, cuts, low, top_value):
    gain = 1.0
    for dim, shards_of in cuts:
        draws = jax.random.uniform(jax.random.fold_in(jax.random.fold_in(rng, 6), dim), (shards_of,), jnp.float32, low / len(cuts), top_value / len(cuts))
        gain = gain * jnp.repeat(jnp.exp(draws), dims[dim] // shards_of).reshape((-1,) + (1,) * (len(dims) - 1 - dim))
    return gain


def scatter_about(rng, extent, width, most, split=(), dtype=jnp.bfloat16):
    factor_of = shard_levels(rng, extent, split, -0.22, 0.18) if split else 1.0
    drawn = jax.random.normal(rng, extent, jnp.float32) * width * factor_of
    return jnp.minimum(jnp.maximum(drawn, -most), most).astype(dtype)


def setup_inputs(seed: int = 0) -> dict:
    seeds = jax.random.split(jax.random.key(seed), 14)
    return {
        "queries": draw_queries(jax.random.fold_in(seeds[13], 71), 0),
        "new_latent": scatter_about(seeds[1], (STEPS, REQS, KV), 1.0, 4.0, ((1, 64),)),
        "cache": draw_cache(jax.random.fold_in(seeds[13], 71), 0),
        "lengths": draw_lengths(jax.random.fold_in(seeds[13], 71), 0),
        "hidden_in": scatter_about(seeds[4], (STEPS, REQS, D), 0.5, 4.0, ((1, 64),)),
        "norm_gain": jnp.clip(1.0 + 0.18 * jax.random.normal(seeds[5], (D,), jnp.float32), 0.1, 1.9),
        "uv_weight": scatter_about(seeds[6], (HEADS, LAT, VH), LAT ** -0.5, 0.25),
        "out_weight": scatter_about(seeds[7], (HEADS * VH, D), (HEADS * VH) ** -0.5, 0.1875),
        "expert_ids": draw_expert_ids(jax.random.fold_in(seeds[13], 71), 0),
        "gate_weight": jnp.clip(0.049804688 + 0.54785156 * jax.random.uniform(seeds[9], (STEPS, REQS, TOPK), jnp.float32) ** shard_levels(seeds[9], (STEPS, REQS, TOPK), ((1, 64),), -0.2, 0.2), 0.049804688, 0.59765625).astype(jnp.bfloat16),
        "capacity": draw_capacity(jax.random.fold_in(seeds[13], 71), 0),
        "gate_up": scatter_about(seeds[11], (SPECIALIST_POOL, D, 2 * FF), D ** -0.5, 0.125, ((0, 64),)),
        "down": scatter_about(seeds[12], (SPECIALIST_POOL, FF, D), FF ** -0.5, 0.15625, ((0, 64),)),
    }


def run_expert(inputs):
    rows_in, gate_up_one, down_one = inputs
    both = jnp.dot(rows_in, gate_up_one, preferred_element_type=jnp.float32)
    active = (jax.nn.silu(both[:, :FF]) * both[:, FF:]).astype(jnp.bfloat16)
    return jnp.dot(active, down_one, preferred_element_type=jnp.float32).astype(jnp.bfloat16)

def reference(queries, new_latent, cache, lengths, hidden_in, norm_gain, uv_weight, out_weight, expert_ids, gate_weight, capacity, gate_up, down):
    score_scale = (QKNOPE + ROPE) ** (-0.5)
    batch_rows = REQ_DEV // MICRO
    groups = REQS // batch_rows
    cache_wide = cache.astype(jnp.float32)
    open_keys = jnp.arange(CTX)[None, :] < lengths[:, None]
    uv_wide = uv_weight.astype(jnp.float32)
    results = []
    for step_index in range(STEPS):
        query = queries[step_index].astype(jnp.float32)
        new_keys = new_latent[:step_index + 1].astype(jnp.float32)
        old_score = jnp.einsum('rhc,rtc->rht', query, cache_wide) * score_scale
        old_score = jnp.where(open_keys[:, None, :], old_score, -jnp.inf)
        new_score = jnp.einsum('rhc,urc->rhu', query, new_keys) * score_scale
        row_top = jnp.maximum(lax.optimization_barrier(jnp.max(old_score, axis=2)), lax.optimization_barrier(jnp.max(new_score, axis=2)))
        old_exp = jnp.exp(old_score - row_top[:, :, None])
        new_exp = jnp.exp(new_score - row_top[:, :, None])
        denom_sum = lax.optimization_barrier(jnp.sum(old_exp, axis=2)) + lax.optimization_barrier(jnp.sum(new_exp, axis=2))
        old_weight = lax.optimization_barrier(old_exp.astype(jnp.bfloat16)).astype(jnp.float32)
        new_weight = lax.optimization_barrier(new_exp.astype(jnp.bfloat16)).astype(jnp.float32)
        latent = jnp.einsum('rht,rtl->rhl', old_weight, cache_wide[:, :, :LAT])
        latent = latent + jnp.einsum('rhu,url->rhl', new_weight, new_keys[:, :, :LAT])
        latent = (latent / denom_sum[:, :, None]).astype(jnp.bfloat16)
        heads_out = jnp.einsum('rhl,hlv->rhv', latent.astype(jnp.float32), uv_wide).astype(jnp.bfloat16)
        residual = hidden_in[step_index].astype(jnp.float32) + jnp.dot(heads_out.reshape(REQS, HEADS * VH), out_weight, preferred_element_type=jnp.float32)
        normed = (residual * lax.rsqrt(lax.optimization_barrier(jnp.mean(residual * residual, axis=1, keepdims=True)) + 1e-06) * norm_gain).astype(jnp.bfloat16)
        picked = expert_ids[step_index].reshape(groups, batch_rows, TOPK)
        onehot = (picked[:, :, :, None] == jnp.arange(SPECIALIST_POOL)[None, None, None, :]).astype(jnp.int32)
        counts = lax.optimization_barrier(jnp.sum(onehot, axis=2))
        before = jnp.cumsum(counts, axis=1) - counts
        retained = (counts > 0) & (before < capacity[None, None, :])
        gate_rows = gate_weight[step_index].reshape(groups, batch_rows, TOPK).astype(jnp.float32)
        gate_sum = lax.optimization_barrier(jnp.sum(onehot.astype(jnp.float32) * gate_rows[:, :, :, None], axis=2))
        slot_hit = (retained[:, :, :, None] & (before[:, :, :, None] == jnp.arange(CAP)[None, None, None, :])).astype(jnp.float32)
        normed_wide = normed.reshape(groups, batch_rows, D).astype(jnp.float32)
        buffer = jnp.einsum('gbec,gbd->egcd', slot_hit, normed_wide).astype(jnp.bfloat16)
        buffer = buffer.reshape(SPECIALIST_POOL, groups * CAP, D)
        expert_out = lax.map(run_expert, (buffer, gate_up, down))
        expert_wide = expert_out.reshape(SPECIALIST_POOL, groups, CAP, D).astype(jnp.float32)
        moe = jnp.einsum('gbec,egcd->gbd', slot_hit * gate_sum[:, :, :, None], expert_wide)
        results.append((residual + moe.reshape(REQS, D)).astype(jnp.bfloat16))
    return jnp.stack(results)
```

```python
import functools

import jax
import jax.numpy as jnp
from jax import lax
from jax.experimental import pallas as pl
from jax.experimental.pallas import tpu as pltpu
from jax.sharding import PartitionSpec as P

LAT = 512
ROPE = 64
QKNOPE = 128
CAP = 3
MICRO = 2
CHUNKS = 1
ROWS = 24
F32 = jnp.float32
BF16 = jnp.bfloat16
MIB = 1024 * 1024


def iota(shape, dim):
    return lax.broadcasted_iota(jnp.int32, shape, dim)


def dot(a, b, contract=((1,), (0,))):
    return lax.dot_general(a, b, (contract, ((), ())), preferred_element_type=F32)


def attend_kernel(
    pool_ref, len_ref, q_ref, nl_ref, cache_ref, hid_ref, gain_ref, uv_ref, ow_hbm, ids_ref, gw_ref, cap_ref,
    *rest,
):
    outs = rest[: 3 * CHUNKS]
    mixed_ref, lat_sc, ow_sc, ow_sem = rest[3 * CHUNKS :]
    fetch = pltpu.make_async_copy(ow_hbm, ow_sc, ow_sem)
    fetch.start()
    pool = pool_ref[0]
    steps, reqs, heads, width = q_ref.shape
    ctx = cache_ref.shape[1]
    model = hid_ref.shape[2]
    experts = cap_ref.shape[1]
    tokens = steps * reqs
    per_req = steps * heads
    scale = (QKNOPE + ROPE) ** (-0.5)

    def mine(ref):
        wide = ref[...].astype(F32) if ref.dtype != jnp.int32 else ref[...]
        part = jnp.where(pool == 0, wide[:, :reqs], wide[:, reqs:])
        return part.reshape(tokens, wide.shape[2])

    fresh = mine(nl_ref).astype(BF16)
    q_rows = [q_ref[:, r].astype(F32).reshape(per_req, width).astype(BF16) for r in range(reqs)]
    position = iota((per_req, ctx), 1)
    old = []
    for r in range(reqs):
        s = dot(q_rows[r], cache_ref[r], ((1,), (1,))) * scale
        old.append(jnp.where(position < len_ref[pool * reqs + r], s, -jnp.inf))
    old = jnp.concatenate(old, axis=0)
    new = dot(jnp.concatenate(q_rows, axis=0), fresh, ((1,), (1,))) * scale
    row = iota(new.shape, 0)
    col = iota(new.shape, 1)
    valid = (row // per_req == col % reqs) & (col // reqs <= (row // heads) % steps)
    new = jnp.where(valid, new, -jnp.inf)
    top = jnp.maximum(jnp.max(old, axis=1, keepdims=True), jnp.max(new, axis=1, keepdims=True))
    old = jnp.exp(old - top)
    new = jnp.exp(new - top)
    total = jnp.sum(old, axis=1, keepdims=True) + jnp.sum(new, axis=1, keepdims=True)
    old = old.astype(BF16)
    latent = jnp.concatenate(
        [dot(old[r * per_req : (r + 1) * per_req], cache_ref[r, :, :LAT]) for r in range(reqs)], axis=0
    )
    latent = latent + dot(new.astype(BF16), fresh[:, :LAT])
    latent = latent / total
    for i in range(lat_sc.shape[0]):
        lat_sc[i] = latent[:, i * 128 : (i + 1) * 128]
    head_out = []
    for h in range(heads):
        rows = [
            jnp.concatenate(
                [lat_sc[i, pl.ds(s * heads + h, reqs, stride=per_req), :] for i in range(lat_sc.shape[0])],
                axis=1,
            )
            for s in range(steps)
        ]
        lat_h = jnp.concatenate(rows, axis=0).astype(BF16)
        head_out.append(dot(lat_h, uv_ref[h]).astype(BF16))
    head_out = jnp.concatenate(head_out, axis=1)

    ids = mine(ids_ref)
    gates = mine(gw_ref)
    lane = iota((tokens, experts), 1)
    named = jnp.zeros((tokens, experts), F32)
    gate = jnp.zeros((tokens, experts), F32)
    for k in range(ids.shape[1]):
        hit = ids[:, k : k + 1] == lane
        named = named + hit.astype(F32)
        gate = gate + jnp.where(hit, gates[:, k : k + 1], 0.0)
    a, b = iota((tokens, tokens), 0), iota((tokens, tokens), 1)
    earlier = ((a // reqs == b // reqs) & (b < a)).astype(BF16)
    before = dot(earlier, named.astype(BF16))
    kept = (named > 0) & (before < cap_ref[...].astype(F32))
    per_chunk = tokens // CHUNKS
    slots = CAP * steps // CHUNKS
    parts = ROWS // slots
    step_in_chunk = (iota((tokens, experts), 0) % per_chunk) // reqs
    slot = jnp.where(kept, step_in_chunk.astype(F32) * CAP + before, -100.0)

    fetch.wait()
    mixed = mine(hid_ref) + dot(head_out, ow_sc[...])
    mixed_ref[...] = mixed
    normed = (
        mixed * lax.rsqrt(jnp.mean(mixed * mixed, axis=1, keepdims=True) + 1e-06) * gain_ref[...]
    ).astype(BF16)

    lanes = parts * per_chunk
    spread = (iota((per_chunk, lanes), 1) % per_chunk == iota((per_chunk, lanes), 0)).astype(BF16)
    offset = (iota((experts, lanes), 1) // per_chunk * slots).astype(F32)
    wide = model // parts
    for c in range(CHUNKS):
        x_ref, at_ref, gate_ref = outs[3 * c : 3 * c + 3]
        rows = slice(c * per_chunk, (c + 1) * per_chunk)
        at = dot(slot[rows].astype(BF16), spread, ((0,), (0,))) + offset
        at_ref[...] = at
        gate_ref[...] = dot(gate[rows].astype(BF16), spread, ((0,), (0,)))
        stacked = jnp.concatenate(
            [normed[rows, i * wide : (i + 1) * wide] for i in range(parts)], axis=0
        )
        some = 16
        for e in range(0, experts, some):
            place = (iota((some, ROWS, lanes), 1).astype(F32) == at[e : e + some][:, None, :]).astype(F32)
            place = place.reshape(some * ROWS, lanes).astype(BF16)
            x_ref[e * ROWS : (e + some) * ROWS, :] = dot(place, stacked).astype(BF16)


def attend(pool, lengths, queries, new_latent, cache, hidden_in, gain, uv, ow, ids, gates, capacity):
    steps, demand, heads, width = queries.shape
    reqs = demand // MICRO
    model = hidden_in.shape[2]
    experts = capacity.shape[1]
    tokens = steps * reqs
    per_chunk = tokens // CHUNKS
    parts = ROWS // (CAP * steps // CHUNKS)
    lanes = parts * per_chunk
    outs = []
    for _ in range(CHUNKS):
        outs += [
            jax.ShapeDtypeStruct((experts * ROWS, model // parts), BF16),
            jax.ShapeDtypeStruct((experts, lanes), F32),
            jax.ShapeDtypeStruct((experts, lanes), F32),
        ]
    outs.append(jax.ShapeDtypeStruct((tokens, model), F32))
    full = lambda a: pl.BlockSpec(a.shape, lambda i, p: (0,) * a.ndim)
    return pl.pallas_call(
        attend_kernel,
        out_shape=outs,
        grid_spec=pltpu.PrefetchScalarGridSpec(
            num_scalar_prefetch=1,
            grid=(1,),
            in_specs=[
                pl.BlockSpec(memory_space=pltpu.SMEM),
                pl.BlockSpec((steps, reqs, heads, width), lambda i, p: (0, p[0], 0, 0)),
                full(new_latent),
                pl.BlockSpec((reqs,) + cache.shape[1:], lambda i, p: (p[0], 0, 0)),
                full(hidden_in),
                full(gain),
                full(uv),
                pl.BlockSpec(memory_space=pl.ANY),
                full(ids),
                full(gates),
                full(capacity),
            ],
            out_specs=[full(o) for o in outs],
            scratch_shapes=[
                pltpu.VMEM((LAT // 128, tokens * heads, 128), F32),
                pltpu.VMEM(ow.shape, BF16),
                pltpu.SemaphoreType.DMA,
            ],
        ),
        compiler_params=pltpu.CompilerParams(vmem_limit_bytes=48 * MIB),
        name="attend",
    )(pool, lengths, queries, new_latent, cache, hidden_in, gain, uv, ow, ids, gates, capacity)


GROUP = 8


def order_matrix(slots):
    n = GROUP * ROWS
    o, i = iota((n, n), 0), iota((n, n), 1)
    per_part = GROUP * slots
    source = (o % per_part) // slots
    want = source * ROWS + (o // per_part) * slots + o % slots
    return (want == i).astype(BF16)


def serve_kernel(x_ref, gate_ref, up_ref, down_hbm, y_ref, rows_sc, act_sc, down_sc, y_sc, sem):
    step = pl.program_id(0)
    n_rows, model = rows_sc.shape
    wide = x_ref.shape[1]
    parts = model // wide
    slots = ROWS // parts
    n = GROUP * ROWS
    per_part = GROUP * slots
    groups = x_ref.shape[0] // n
    fetch = pltpu.make_async_copy(down_hbm, down_sc, sem)

    @pl.when(step == 0)
    def _():
        fetch.start()
        order = order_matrix(slots)
        for g in range(groups):
            got = dot(order, x_ref[g * n : (g + 1) * n, :]).astype(BF16)
            for i in range(parts):
                rows_sc[g * per_part : (g + 1) * per_part, i * wide : (i + 1) * wide] = got[
                    i * per_part : (i + 1) * per_part
                ]

    cols = gate_ref.shape[2]
    weight = jnp.concatenate([gate_ref[0], up_ref[0]], axis=1)
    both = dot(rows_sc[...], weight)
    gate = both[:, :cols]
    act = gate / (1.0 + jnp.exp(-gate)) * both[:, cols:]
    act_sc[step] = act.astype(BF16)

    @pl.when(step == pl.num_programs(0) - 1)
    def _():
        fetch.wait()
        act_all = jnp.concatenate([act_sc[i] for i in range(act_sc.shape[0])], axis=1)
        block = 256
        for i in range(model // block):
            y_sc[:, i * block : (i + 1) * block] = dot(
                act_all, down_sc[:, i * block : (i + 1) * block]
            ).astype(BF16)
        order = order_matrix(slots)
        for g in range(groups):
            piece = jnp.concatenate(
                [
                    y_sc[g * per_part : (g + 1) * per_part, i * wide : (i + 1) * wide]
                    for i in range(parts)
                ],
                axis=0,
            )
            y_ref[g * n : (g + 1) * n, :] = dot(order, piece, ((0,), (0,))).astype(BF16)


def serve(x, gate_up, down):
    n_in, wide = x.shape
    _, model, twice = gate_up.shape
    hidden = twice // 2
    cols = 128
    count = hidden // cols
    n_rows = n_in * wide // model
    return pl.pallas_call(
        serve_kernel,
        out_shape=jax.ShapeDtypeStruct((n_in, wide), BF16),
        grid=(count,),
        in_specs=[
            pl.BlockSpec((n_in, wide), lambda i: (0, 0)),
            pl.BlockSpec((1, model, cols), lambda i: (0, 0, i)),
            pl.BlockSpec((1, model, cols), lambda i: (0, 0, i + count)),
            pl.BlockSpec(memory_space=pl.ANY),
        ],
        out_specs=pl.BlockSpec((n_in, wide), lambda i: (0, 0)),
        scratch_shapes=[
            pltpu.VMEM((n_rows, model), BF16),
            pltpu.VMEM((count, n_rows, cols), BF16),
            pltpu.VMEM(down.shape[1:], BF16),
            pltpu.VMEM((n_rows, model), BF16),
            pltpu.SemaphoreType.DMA,
        ],
        compiler_params=pltpu.CompilerParams(vmem_limit_bytes=48 * MIB),
        name="serve",
    )(x, gate_up, gate_up, down[0])


def combine_kernel(pool_ref, at_ref, gate_ref, y_ref, mixed_ref, keep_ref, give_ref):
    experts, lanes = at_ref.shape
    tokens, model = mixed_ref.shape
    parts = lanes // tokens
    wide = model // parts
    some = 16
    acc = jnp.zeros((lanes, wide), F32)
    for e in range(0, experts, some):
        hit = iota((some, ROWS, lanes), 1).astype(F32) == at_ref[e : e + some][:, None, :]
        weight = jnp.where(hit, gate_ref[e : e + some][:, None, :], 0.0)
        weight = weight.reshape(some * ROWS, lanes).astype(BF16)
        acc = acc + dot(weight, y_ref[e * ROWS : (e + some) * ROWS, :], ((0,), (0,)))
    moe = jnp.concatenate([acc[i * tokens : (i + 1) * tokens] for i in range(parts)], axis=1)
    out = (mixed_ref[...] + moe)
    first, second = out[:, : model // 2], out[:, model // 2 :]
    lower = pool_ref[0] == 0
    keep_ref[...] = jnp.where(lower, first, second).astype(BF16)
    give_ref[...] = jnp.where(lower, second, first).astype(BF16)


def combine(pool, at, gate, y, mixed, chunk):
    tokens = mixed.shape[0] // CHUNKS
    model = mixed.shape[1]
    full = lambda a: pl.BlockSpec(a.shape, lambda i, p: (0,) * a.ndim)
    half = jax.ShapeDtypeStruct((tokens, model // 2), BF16)
    return pl.pallas_call(
        combine_kernel,
        out_shape=[half, half],
        grid_spec=pltpu.PrefetchScalarGridSpec(
            num_scalar_prefetch=1,
            grid=(1,),
            in_specs=[full(at), full(gate), full(y), pl.BlockSpec((tokens, model), lambda i, p: (chunk, 0))],
            out_specs=[full(half), full(half)],
        ),
        compiler_params=pltpu.CompilerParams(vmem_limit_bytes=48 * MIB),
        name="combine",
    )(pool, at, gate, y, mixed)


def body(
    queries,
    new_latent,
    cache,
    lengths,
    hidden_in,
    norm_gain,
    uv_weight,
    out_weight,
    expert_ids,
    gate_weight,
    capacity,
    gate_up,
    down,
):
    steps, demand = queries.shape[:2]
    reqs = demand // MICRO
    model = hidden_in.shape[2]
    pool = lax.axis_index("pool")
    pool_arr = jnp.full((1,), pool, jnp.int32)
    found = attend(
        pool_arr, lengths, queries, new_latent, cache, hidden_in, norm_gain[None, :], uv_weight, out_weight,
        expert_ids, gate_weight, capacity[None, :],
    )
    mixed = found[-1]
    trade = functools.partial(
        lax.all_to_all, axis_name="dev", split_axis=0, concat_axis=0, tiled=True
    )
    arrived = [trade(found[3 * c]) for c in range(CHUNKS)]
    returned = [trade(serve(x, gate_up, down)) for x in arrived]
    halves = []
    for c in range(CHUNKS):
        keep, give = combine(pool_arr, found[3 * c + 1], found[3 * c + 2], returned[c], mixed, c)
        got = lax.ppermute(give, "pool", [(0, 1), (1, 0)])
        keep = keep.reshape(steps // CHUNKS, reqs, model // 2)
        got = got.reshape(steps // CHUNKS, reqs, model // 2)
        halves.append(
            jnp.where(
                pool == 0,
                jnp.concatenate([keep, got], axis=1),
                jnp.concatenate([got, keep], axis=1),
            )
        )
    return jnp.concatenate(halves, axis=0)


def solution(mesh):
    in_specs = (
        P(None, "dev", None, None),
        P(None, "dev", None),
        P("dev", None, None),
        P("dev"),
        P(None, "dev", None),
        P(),
        P(),
        P(),
        P(None, "dev", None),
        P(None, "dev", None),
        P(),
        P("dev", None, None),
        P("dev", None, None),
    )
    out_specs = P(None, "dev", "pool")
    return jax.shard_map(body, mesh=mesh, in_specs=in_specs, out_specs=out_specs, check_vma=False)
```

```python
import functools

import jax
import jax.numpy as jnp
from jax import lax
from jax.experimental import pallas as pl
from jax.experimental.pallas import tpu as pltpu
from jax.sharding import PartitionSpec as P

LAT = 512
ROPE = 64
QKNOPE = 128
CAP = 3
MICRO = 2
ROWS = 24
F32 = jnp.float32
BF16 = jnp.bfloat16
MIB = 1024 * 1024
SERVE_MIB = 40


def iota(shape, dim):
    return lax.broadcasted_iota(jnp.int32, shape, dim)


def dot(a, b, contract=((1,), (0,))):
    return lax.dot_general(a, b, (contract, ((), ())), preferred_element_type=F32)


def attend_kernel(
    pool_ref, len_hbm, q_hbm, nl_hbm, cache_hbm, hid_hbm, gain_hbm, uv_hbm, ow_hbm, ids_hbm, gw_hbm, cap_hbm,
    x_ref, at_ref, gate_ref, mixed_ref,
    len_sc, q_sc, nl_sc, cache_sc, hid_sc, gain_sc, uv_sc, ow_sc, ids_sc, gw_sc, cap_sc, lat_sc, sem,
):
    pool = pool_ref[0]
    steps, reqs, heads, width = q_sc.shape
    ctx = cache_sc.shape[2]
    model = hid_sc.shape[2]
    experts = cap_sc.shape[1]
    tokens = steps * reqs
    per_req = steps * heads
    scale = (QKNOPE + ROPE) ** (-0.5)

    half = pl.ds(pool * reqs, reqs)
    moves = {}
    for i, (name, src, dst) in enumerate((
        ("len", len_hbm, len_sc),
        ("q", q_hbm.at[:, half], q_sc),
        ("nl", nl_hbm, nl_sc),
        ("cache", cache_hbm.at[half], cache_sc),
        ("ids", ids_hbm, ids_sc),
        ("gw", gw_hbm, gw_sc),
        ("cap", cap_hbm, cap_sc),
        ("uv", uv_hbm, uv_sc),
        ("hid", hid_hbm, hid_sc),
        ("gain", gain_hbm, gain_sc),
        ("ow", ow_hbm, ow_sc),
    )):
        moves[name] = pltpu.make_async_copy(src, dst, sem.at[i])
        moves[name].start()

    def mine(ref):
        wide = ref[...].astype(F32)
        part = jnp.where(pool == 0, wide[:, :reqs], wide[:, reqs:])
        return part.reshape(tokens, wide.shape[2])

    for name in ("len", "q", "nl", "ids", "gw", "cap"):
        moves[name].wait()
    demand = ids_sc.shape[2]
    cap_row = cap_sc[...].astype(F32)
    diagonal = iota((experts, experts), 0) == iota((experts, experts), 1)
    cap = jnp.sum(jnp.where(diagonal, cap_row, 0.0), axis=1, keepdims=True)
    ids = ids_sc[...]
    gates = gw_sc[...].astype(F32)
    mark = iota((experts, demand), 0)
    a, b = iota((demand, demand), 0), iota((demand, demand), 1)
    earlier = ((a // reqs == b // reqs) & (a < b)).astype(BF16)
    slots = CAP * steps
    parts = ROWS // slots
    lanes = parts * tokens
    row, lane = iota((demand, lanes), 0), iota((demand, lanes), 1)
    at = (iota((experts, lanes), 1) // tokens * slots).astype(F32)
    gate_of = jnp.zeros((experts, lanes), F32)
    for s in range(steps):
        named = jnp.zeros((experts, demand), F32)
        gate = jnp.zeros((experts, demand), F32)
        for k in range(ids.shape[0]):
            hit = ids[k, s : s + 1] == mark
            named = named + hit.astype(F32)
            gate = gate + jnp.where(hit, gates[k, s : s + 1], 0.0)
        before = dot(named.astype(BF16), earlier)
        slot = jnp.where((named > 0) & (before < cap), before + s * CAP, -100.0)
        spread = ((lane % tokens == s * reqs + row % reqs) & (row // reqs == pool)).astype(BF16)
        at = at + dot(slot.astype(BF16), spread)
        gate_of = gate_of + dot(gate.astype(BF16), spread)
    at_ref[...] = at
    gate_ref[...] = gate_of

    fresh = mine(nl_sc).astype(BF16)
    q_rows = [q_sc[:, r].astype(F32).reshape(per_req, width).astype(BF16) for r in range(reqs)]
    new = dot(jnp.concatenate(q_rows, axis=0), fresh, ((1,), (1,))) * scale
    row = iota(new.shape, 0)
    col = iota(new.shape, 1)
    valid = (row // per_req == col % reqs) & (col // reqs <= (row // heads) % steps)
    new = jnp.where(valid, new, -jnp.inf)
    moves["cache"].wait()
    position = iota((per_req, ctx), 1)
    old = []
    for r in range(reqs):
        score = dot(q_rows[r], cache_sc[r]) * scale
        old.append(jnp.where(position < len_sc[pool * reqs + r], score, -jnp.inf))
    old = jnp.concatenate(old, axis=0)
    top = jnp.maximum(jnp.max(old, axis=1, keepdims=True), jnp.max(new, axis=1, keepdims=True))
    old = jnp.exp(old - top)
    new = jnp.exp(new - top)
    total = jnp.sum(old, axis=1, keepdims=True) + jnp.sum(new, axis=1, keepdims=True)
    old = old.astype(BF16)
    latent = jnp.concatenate(
        [
            dot(old[r * per_req : (r + 1) * per_req], cache_sc[r, :LAT, :], ((1,), (1,)))
            for r in range(reqs)
        ],
        axis=0,
    )
    latent = latent + dot(new.astype(BF16), fresh[:, :LAT])
    latent = latent / total
    for i in range(lat_sc.shape[0]):
        lat_sc[i] = latent[:, i * 128 : (i + 1) * 128]
    moves["uv"].wait()
    head_out = []
    for h in range(heads):
        rows = [
            jnp.concatenate(
                [lat_sc[i, pl.ds(s * heads + h, reqs, stride=per_req), :] for i in range(lat_sc.shape[0])],
                axis=1,
            )
            for s in range(steps)
        ]
        lat_h = jnp.concatenate(rows, axis=0).astype(BF16)
        head_out.append(dot(lat_h, uv_sc[h]).astype(BF16))
    head_out = jnp.concatenate(head_out, axis=1)
    for name in ("hid", "gain", "ow"):
        moves[name].wait()
    mixed = mine(hid_sc) + dot(head_out, ow_sc[...])
    mixed_ref[...] = mixed
    normed = (
        mixed * lax.rsqrt(jnp.mean(mixed * mixed, axis=1, keepdims=True) + 1e-06) * gain_sc[...]
    ).astype(BF16)

    wide = model // parts
    stacked = jnp.concatenate([normed[:, i * wide : (i + 1) * wide] for i in range(parts)], axis=0)
    some = 16
    for e in range(0, experts, some):
        place = (iota((some, ROWS, lanes), 1).astype(F32) == at[e : e + some][:, None, :]).astype(F32)
        place = place.reshape(some * ROWS, lanes).astype(BF16)
        x_ref[e * ROWS : (e + some) * ROWS, :] = dot(place, stacked).astype(BF16)


def attend(pool, lengths, queries, new_latent, cache, hidden_in, gain, uv, ow, ids, gates, capacity):
    steps, demand, heads, width = queries.shape
    reqs = demand // MICRO
    model = hidden_in.shape[2]
    experts = capacity.shape[1]
    tokens = steps * reqs
    parts = ROWS // (CAP * steps)
    lanes = parts * tokens
    outs = [
        jax.ShapeDtypeStruct((experts * ROWS, model // parts), BF16),
        jax.ShapeDtypeStruct((experts, lanes), F32),
        jax.ShapeDtypeStruct((experts, lanes), F32),
        jax.ShapeDtypeStruct((tokens, model), F32),
    ]
    full = lambda a: pl.BlockSpec(a.shape, lambda i, p: (0,) * a.ndim)
    inputs = (lengths, queries, new_latent, cache, hidden_in, gain, uv, ow, ids, gates, capacity)
    like = lambda a: pltpu.VMEM(a.shape, a.dtype)
    return pl.pallas_call(
        attend_kernel,
        out_shape=outs,
        grid_spec=pltpu.PrefetchScalarGridSpec(
            num_scalar_prefetch=1,
            grid=(1,),
            in_specs=[pl.BlockSpec(memory_space=pltpu.HBM)] * len(inputs),
            out_specs=[full(o) for o in outs],
            scratch_shapes=[
                pltpu.SMEM(lengths.shape, lengths.dtype),
                pltpu.VMEM((steps, reqs, heads, width), BF16),
                like(new_latent),
                pltpu.VMEM((reqs,) + cache.shape[1:], BF16),
                like(hidden_in),
                like(gain),
                like(uv),
                like(ow),
                like(ids),
                like(gates),
                like(capacity),
                pltpu.VMEM((LAT // 128, tokens * heads, 128), F32),
                pltpu.SemaphoreType.DMA((len(inputs),)),
            ],
        ),
        compiler_params=pltpu.CompilerParams(vmem_limit_bytes=60 * MIB),
        name="attend",
    )(pool, *inputs)


GROUP = 8


def order_matrix(slots):
    n = GROUP * ROWS
    o, i = iota((n, n), 0), iota((n, n), 1)
    per_part = GROUP * slots
    source = (o % per_part) // slots
    want = source * ROWS + (o // per_part) * slots + o % slots
    return (want == i).astype(BF16)


def serve_kernel(x_ref, gate_up_hbm, down_ref, warm_ref, y_ref, rows_sc, act_sc, y_sc, weight_sc, sem):
    model = rows_sc.shape[1]
    wide = x_ref.shape[1]
    parts = model // wide
    slots = ROWS // parts
    n = GROUP * ROWS
    per_part = GROUP * slots
    groups = x_ref.shape[0] // n
    hidden = down_ref.shape[0]
    block = 256
    columns = [(c, min(block, hidden - c)) for c in range(0, hidden, block)]
    moves = []
    for k, (c, w) in enumerate(columns):
        for i in range(2):
            moves.append(
                pltpu.make_async_copy(
                    gate_up_hbm.at[0, :, pl.ds(i * hidden + c, w)],
                    weight_sc.at[k % 3, :, pl.ds(i * w, w)],
                    sem.at[k % 3, i],
                )
            )

    def begin(k):
        if k < len(columns):
            moves[2 * k].start()
            moves[2 * k + 1].start()

    begin(0)
    begin(1)
    order = order_matrix(slots)
    for g in range(groups):
        got = dot(order, x_ref[g * n : (g + 1) * n, :]).astype(BF16)
        for i in range(parts):
            rows_sc[g * per_part : (g + 1) * per_part, i * wide : (i + 1) * wide] = got[
                i * per_part : (i + 1) * per_part
            ]
    for k, (c, w) in enumerate(columns):
        begin(k + 2)
        moves[2 * k].wait()
        moves[2 * k + 1].wait()
        gate = dot(rows_sc[...], weight_sc[k % 3, :, :w])
        up = dot(rows_sc[...], weight_sc[k % 3, :, w : 2 * w])
        act_sc[:, c : c + w] = (gate / (1.0 + jnp.exp(-gate)) * up).astype(BF16)
    for c in range(0, model, block):
        y_sc[:, c : c + block] = dot(act_sc[...], down_ref[:, c : c + block]).astype(BF16)
    for g in range(groups):
        piece = jnp.concatenate(
            [y_sc[g * per_part : (g + 1) * per_part, i * wide : (i + 1) * wide] for i in range(parts)],
            axis=0,
        )
        y_ref[g * n : (g + 1) * n, :] = dot(order, piece, ((0,), (0,))).astype(BF16)


def serve(x, gate_up, down, warm):
    n_in, wide = x.shape
    _, model, twice = gate_up.shape
    n_rows = n_in * wide // model
    vmem = pl.BlockSpec(memory_space=pltpu.VMEM)
    return pl.pallas_call(
        serve_kernel,
        out_shape=jax.ShapeDtypeStruct((n_in, wide), BF16),
        in_specs=[vmem, pl.BlockSpec(memory_space=pl.ANY), vmem, pl.BlockSpec(memory_space=pl.ANY)],
        out_specs=vmem,
        scratch_shapes=[
            pltpu.VMEM((n_rows, model), BF16),
            pltpu.VMEM((n_rows, twice // 2), BF16),
            pltpu.VMEM((n_rows, model), BF16),
            pltpu.VMEM((3, model, 512), BF16),
            pltpu.SemaphoreType.DMA((3, 2)),
        ],
        compiler_params=pltpu.CompilerParams(vmem_limit_bytes=SERVE_MIB * MIB),
        name="serve",
    )(x, gate_up, down[0], warm)


def combine_kernel(pool_ref, at_ref, gate_ref, y_ref, mixed_ref, keep_ref, give_ref):
    experts, lanes = at_ref.shape
    tokens, model = mixed_ref.shape
    parts = lanes // tokens
    wide = model // parts
    some = 16
    acc = jnp.zeros((lanes, wide), F32)
    for e in range(0, experts, some):
        hit = iota((some, ROWS, lanes), 1).astype(F32) == at_ref[e : e + some][:, None, :]
        weight = jnp.where(hit, gate_ref[e : e + some][:, None, :], 0.0)
        weight = weight.reshape(some * ROWS, lanes).astype(BF16)
        acc = acc + dot(weight, y_ref[e * ROWS : (e + some) * ROWS, :], ((0,), (0,)))
    moe = jnp.concatenate([acc[i * tokens : (i + 1) * tokens] for i in range(parts)], axis=1)
    out = (mixed_ref[...] + moe)
    first, second = out[:, : model // 2], out[:, model // 2 :]
    lower = pool_ref[0] == 0
    keep_ref[...] = jnp.where(lower, first, second).astype(BF16)
    give_ref[...] = jnp.where(lower, second, first).astype(BF16)


def combine(pool, at, gate, y, mixed):
    tokens = mixed.shape[0]
    model = mixed.shape[1]
    full = lambda a: pl.BlockSpec(a.shape, lambda i, p: (0,) * a.ndim)
    half = jax.ShapeDtypeStruct((tokens, model // 2), BF16)
    return pl.pallas_call(
        combine_kernel,
        out_shape=[half, half],
        grid_spec=pltpu.PrefetchScalarGridSpec(
            num_scalar_prefetch=1,
            grid=(1,),
            in_specs=[full(at), full(gate), full(y), pl.BlockSpec((tokens, model), lambda i, p: (0, 0))],
            out_specs=[full(half), full(half)],
        ),
        compiler_params=pltpu.CompilerParams(vmem_limit_bytes=16 * MIB),
        name="combine",
    )(pool, at, gate, y, mixed)


def body(
    queries,
    new_latent,
    cache,
    lengths,
    hidden_in,
    norm_gain,
    uv_weight,
    out_weight,
    expert_ids,
    gate_weight,
    capacity,
    gate_up,
    down,
):
    steps, demand = queries.shape[:2]
    reqs = demand // MICRO
    model = hidden_in.shape[2]
    pool = lax.axis_index("pool")
    pool_arr = jnp.full((1,), pool, jnp.int32)
    ring = [(i, (i + 1) % lax.axis_size("dev")) for i in range(lax.axis_size("dev"))]
    warm = lax.ppermute(new_latent[0, :, :128], "dev", ring)
    x, at, gate, mixed = attend(
        pool_arr, lengths, queries, new_latent, jnp.swapaxes(cache, 1, 2), hidden_in, norm_gain[None, :],
        uv_weight, out_weight, jnp.transpose(expert_ids, (2, 0, 1)), jnp.transpose(gate_weight, (2, 0, 1)),
        capacity[None, :],
    )
    x, warm = lax.optimization_barrier((x, warm))
    trade = functools.partial(
        lax.all_to_all, axis_name="dev", split_axis=0, concat_axis=0, tiled=True
    )
    returned = trade(serve(trade(x), gate_up, down, warm))
    keep, give = combine(pool_arr, at, gate, returned, mixed)
    got = lax.ppermute(give, "pool", [(0, 1), (1, 0)])
    keep = keep.reshape(steps, reqs, model // 2)
    got = got.reshape(steps, reqs, model // 2)
    return jnp.where(
        pool == 0, jnp.concatenate([keep, got], axis=1), jnp.concatenate([got, keep], axis=1)
    )


def solution(mesh):
    in_specs = (
        P(None, "dev", None, None),
        P(None, "dev", None),
        P("dev", None, None),
        P("dev"),
        P(None, "dev", None),
        P(),
        P(),
        P(),
        P(None, "dev", None),
        P(None, "dev", None),
        P(),
        P("dev", None, None),
        P("dev", None, None),
    )
    out_specs = P(None, "dev", "pool")
    return jax.shard_map(body, mesh=mesh, in_specs=in_specs, out_specs=out_specs, check_vma=False)
```

```python
import functools

import jax
import jax.numpy as jnp
from jax import lax
from jax.experimental import pallas as pl
from jax.experimental.pallas import tpu as pltpu
from jax.sharding import PartitionSpec as P

LAT = 512
ROPE = 64
QKNOPE = 128
CAP = 3
MICRO = 2
ROWS = 24
F32 = jnp.float32
BF16 = jnp.bfloat16
MIB = 1024 * 1024
ATTEND_MIB = 60
SERVE_MIB = 40


def iota(shape, dim):
    return lax.broadcasted_iota(jnp.int32, shape, dim)


def dot(a, b, contract=((1,), (0,))):
    return lax.dot_general(a, b, (contract, ((), ())), preferred_element_type=F32)


def attend_kernel(
    pool_ref, len_hbm, q_hbm, nl_hbm, cache_hbm, hid_hbm, gain_hbm, uv_hbm, ow_hbm, ids_hbm, gw_hbm, cap_hbm,
    x_ref, at_ref, gate_ref, mixed_ref,
    len_sc, q_sc, nl_sc, cache_sc, hid_sc, gain_sc, uv_sc, ow_sc, ids_sc, gw_sc, cap_sc, lat_sc, sem,
):
    pool = pool_ref[0]
    steps, reqs, heads, width = q_sc.shape
    ctx = cache_sc.shape[2]
    model = hid_sc.shape[2]
    experts = cap_sc.shape[1]
    tokens = steps * reqs
    per_req = steps * heads
    scale = (QKNOPE + ROPE) ** (-0.5)

    half = pl.ds(pool * reqs, reqs)
    moves = {}
    for i, (name, src, dst) in enumerate((
        ("len", len_hbm, len_sc),
        ("q", q_hbm.at[:, half], q_sc),
        ("nl", nl_hbm, nl_sc),
        ("cache", cache_hbm.at[half], cache_sc),
        ("ids", ids_hbm, ids_sc),
        ("gw", gw_hbm, gw_sc),
        ("cap", cap_hbm, cap_sc),
        ("uv", uv_hbm, uv_sc),
        ("hid", hid_hbm, hid_sc),
        ("gain", gain_hbm, gain_sc),
        ("ow", ow_hbm, ow_sc),
    )):
        moves[name] = pltpu.make_async_copy(src, dst, sem.at[i])
        moves[name].start()

    def mine(ref):
        wide = ref[...].astype(F32)
        part = jnp.where(pool == 0, wide[:, :reqs], wide[:, reqs:])
        return part.reshape(tokens, wide.shape[2])

    for name in ("len", "q", "nl", "ids", "gw", "cap"):
        moves[name].wait()
    demand = ids_sc.shape[2]
    cap_row = cap_sc[...].astype(F32)
    diagonal = iota((experts, experts), 0) == iota((experts, experts), 1)
    cap = jnp.sum(jnp.where(diagonal, cap_row, 0.0), axis=1, keepdims=True)
    ids = ids_sc[...]
    gates = gw_sc[...].astype(F32)
    mark = iota((experts, demand), 0)
    a, b = iota((demand, demand), 0), iota((demand, demand), 1)
    earlier = ((a // reqs == b // reqs) & (a < b)).astype(BF16)
    slots = CAP * steps
    parts = ROWS // slots
    lanes = parts * tokens
    row, lane = iota((demand, lanes), 0), iota((demand, lanes), 1)
    at = (iota((experts, lanes), 1) // tokens * slots).astype(F32)
    gate_of = jnp.zeros((experts, lanes), F32)
    for s in range(steps):
        named = jnp.zeros((experts, demand), F32)
        gate = jnp.zeros((experts, demand), F32)
        for k in range(ids.shape[0]):
            hit = ids[k, s : s + 1] == mark
            named = named + hit.astype(F32)
            gate = gate + jnp.where(hit, gates[k, s : s + 1], 0.0)
        before = dot(named.astype(BF16), earlier)
        slot = jnp.where((named > 0) & (before < cap), before + s * CAP, -100.0)
        spread = ((lane % tokens == s * reqs + row % reqs) & (row // reqs == pool)).astype(BF16)
        at = at + dot(slot.astype(BF16), spread)
        gate_of = gate_of + dot(gate.astype(BF16), spread)
    at_ref[...] = at
    gate_ref[...] = gate_of

    fresh = mine(nl_sc).astype(BF16)
    q_rows = [q_sc[:, r].astype(F32).reshape(per_req, width).astype(BF16) for r in range(reqs)]
    new = dot(jnp.concatenate(q_rows, axis=0), fresh, ((1,), (1,))) * scale
    row = iota(new.shape, 0)
    col = iota(new.shape, 1)
    valid = (row // per_req == col % reqs) & (col // reqs <= (row // heads) % steps)
    new = jnp.where(valid, new, -jnp.inf)
    moves["cache"].wait()
    position = iota((per_req, ctx), 1)
    old = []
    for r in range(reqs):
        score = dot(q_rows[r], cache_sc[r]) * scale
        old.append(jnp.where(position < len_sc[pool * reqs + r], score, -jnp.inf))
    old = jnp.concatenate(old, axis=0)
    top = jnp.maximum(jnp.max(old, axis=1, keepdims=True), jnp.max(new, axis=1, keepdims=True))
    old = jnp.exp(old - top)
    new = jnp.exp(new - top)
    total = jnp.sum(old, axis=1, keepdims=True) + jnp.sum(new, axis=1, keepdims=True)
    old = old.astype(BF16)
    latent = jnp.concatenate(
        [
            dot(old[r * per_req : (r + 1) * per_req], cache_sc[r, :LAT, :], ((1,), (1,)))
            for r in range(reqs)
        ],
        axis=0,
    )
    latent = latent + dot(new.astype(BF16), fresh[:, :LAT])
    latent = latent / total
    for i in range(lat_sc.shape[0]):
        lat_sc[i] = latent[:, i * 128 : (i + 1) * 128]
    moves["uv"].wait()
    head_out = []
    for h in range(heads):
        rows = [
            jnp.concatenate(
                [lat_sc[i, pl.ds(s * heads + h, reqs, stride=per_req), :] for i in range(lat_sc.shape[0])],
                axis=1,
            )
            for s in range(steps)
        ]
        lat_h = jnp.concatenate(rows, axis=0).astype(BF16)
        head_out.append(dot(lat_h, uv_sc[h]).astype(BF16))
    head_out = jnp.concatenate(head_out, axis=1)
    for name in ("hid", "gain", "ow"):
        moves[name].wait()
    mixed = mine(hid_sc) + dot(head_out, ow_sc[...])
    mixed_ref[...] = mixed
    normed = (
        mixed * lax.rsqrt(jnp.mean(mixed * mixed, axis=1, keepdims=True) + 1e-06) * gain_sc[...]
    ).astype(BF16)

    wide = model // parts
    stacked = jnp.concatenate([normed[:, i * wide : (i + 1) * wide] for i in range(parts)], axis=0)
    some = 16
    for e in range(0, experts, some):
        place = (iota((some, ROWS, lanes), 1).astype(F32) == at[e : e + some][:, None, :]).astype(F32)
        place = place.reshape(some * ROWS, lanes).astype(BF16)
        x_ref[e * ROWS : (e + some) * ROWS, :] = dot(place, stacked).astype(BF16)


def attend(pool, lengths, queries, new_latent, cache, hidden_in, gain, uv, ow, ids, gates, capacity):
    steps, demand, heads, width = queries.shape
    reqs = demand // MICRO
    model = hidden_in.shape[2]
    experts = capacity.shape[1]
    tokens = steps * reqs
    parts = ROWS // (CAP * steps)
    lanes = parts * tokens
    outs = [
        jax.ShapeDtypeStruct((experts * ROWS, model // parts), BF16),
        jax.ShapeDtypeStruct((experts, lanes), F32),
        jax.ShapeDtypeStruct((experts, lanes), F32),
        jax.ShapeDtypeStruct((tokens, model), F32),
    ]
    full = lambda a: pl.BlockSpec(a.shape, lambda i, p: (0,) * a.ndim)
    inputs = (lengths, queries, new_latent, cache, hidden_in, gain, uv, ow, ids, gates, capacity)
    like = lambda a: pltpu.VMEM(a.shape, a.dtype)
    return pl.pallas_call(
        attend_kernel,
        out_shape=outs,
        grid_spec=pltpu.PrefetchScalarGridSpec(
            num_scalar_prefetch=1,
            grid=(1,),
            in_specs=[pl.BlockSpec(memory_space=pltpu.HBM)] * len(inputs),
            out_specs=[full(o) for o in outs],
            scratch_shapes=[
                pltpu.SMEM(lengths.shape, lengths.dtype),
                pltpu.VMEM((steps, reqs, heads, width), BF16),
                like(new_latent),
                pltpu.VMEM((reqs,) + cache.shape[1:], BF16),
                like(hidden_in),
                like(gain),
                like(uv),
                like(ow),
                like(ids),
                like(gates),
                like(capacity),
                pltpu.VMEM((LAT // 128, tokens * heads, 128), F32),
                pltpu.SemaphoreType.DMA((len(inputs),)),
            ],
        ),
        compiler_params=pltpu.CompilerParams(vmem_limit_bytes=ATTEND_MIB * MIB),
        name="attend",
    )(pool, *inputs)


GROUP = 8


def order_matrix(slots):
    n = GROUP * ROWS
    o, i = iota((n, n), 0), iota((n, n), 1)
    per_part = GROUP * slots
    source = (o % per_part) // slots
    want = source * ROWS + (o // per_part) * slots + o % slots
    return (want == i).astype(BF16)


def serve_kernel(x_ref, gate_up_hbm, down_ref, y_ref, rows_sc, act_sc, y_sc, weight_sc, sem):
    model = rows_sc.shape[1]
    wide = x_ref.shape[1]
    parts = model // wide
    slots = ROWS // parts
    n = GROUP * ROWS
    per_part = GROUP * slots
    groups = x_ref.shape[0] // n
    hidden = down_ref.shape[0]
    block = 256
    columns = [(c, min(block, hidden - c)) for c in range(0, hidden, block)]
    moves = []
    for k, (c, w) in enumerate(columns):
        for i in range(2):
            moves.append(
                pltpu.make_async_copy(
                    gate_up_hbm.at[0, :, pl.ds(i * hidden + c, w)],
                    weight_sc.at[k % 3, :, pl.ds(i * w, w)],
                    sem.at[k % 3, i],
                )
            )

    def begin(k):
        if k < len(columns):
            moves[2 * k].start()
            moves[2 * k + 1].start()

    begin(0)
    begin(1)
    order = order_matrix(slots)
    for g in range(groups):
        got = dot(order, x_ref[g * n : (g + 1) * n, :]).astype(BF16)
        for i in range(parts):
            rows_sc[g * per_part : (g + 1) * per_part, i * wide : (i + 1) * wide] = got[
                i * per_part : (i + 1) * per_part
            ]
    def activate(c, w, gate, up):
        act_sc[:, c : c + w] = (gate / (1.0 + jnp.exp(-gate)) * up).astype(BF16)

    last = None
    for k, (c, w) in enumerate(columns):
        begin(k + 2)
        moves[2 * k].wait()
        moves[2 * k + 1].wait()
        gate = dot(rows_sc[...], weight_sc[k % 3, :, :w])
        up = dot(rows_sc[...], weight_sc[k % 3, :, w : 2 * w])
        if last is not None:
            activate(*last)
        last = (c, w, gate, up)
    activate(*last)
    for c in range(0, model, block):
        y_sc[:, c : c + block] = dot(act_sc[...], down_ref[:, c : c + block]).astype(BF16)
    for g in range(groups):
        piece = jnp.concatenate(
            [y_sc[g * per_part : (g + 1) * per_part, i * wide : (i + 1) * wide] for i in range(parts)],
            axis=0,
        )
        y_ref[g * n : (g + 1) * n, :] = dot(order, piece, ((0,), (0,))).astype(BF16)


def serve(x, gate_up, down):
    n_in, wide = x.shape
    _, model, twice = gate_up.shape
    n_rows = n_in * wide // model
    vmem = pl.BlockSpec(memory_space=pltpu.VMEM)
    return pl.pallas_call(
        serve_kernel,
        out_shape=jax.ShapeDtypeStruct((n_in, wide), BF16),
        in_specs=[vmem, pl.BlockSpec(memory_space=pl.ANY), vmem],
        out_specs=vmem,
        scratch_shapes=[
            pltpu.VMEM((n_rows, model), BF16),
            pltpu.VMEM((n_rows, twice // 2), BF16),
            pltpu.VMEM((n_rows, model), BF16),
            pltpu.VMEM((3, model, 512), BF16),
            pltpu.SemaphoreType.DMA((3, 2)),
        ],
        compiler_params=pltpu.CompilerParams(vmem_limit_bytes=SERVE_MIB * MIB),
        name="serve",
    )(x, gate_up, down[0])


def combine_kernel(pool_ref, at_ref, gate_ref, y_ref, mixed_ref, keep_ref, give_ref):
    experts, lanes = at_ref.shape
    tokens, model = mixed_ref.shape
    parts = lanes // tokens
    wide = model // parts
    some = 16
    acc = jnp.zeros((lanes, wide), F32)
    for e in range(0, experts, some):
        hit = iota((some, ROWS, lanes), 1).astype(F32) == at_ref[e : e + some][:, None, :]
        weight = jnp.where(hit, gate_ref[e : e + some][:, None, :], 0.0)
        weight = weight.reshape(some * ROWS, lanes).astype(BF16)
        acc = acc + dot(weight, y_ref[e * ROWS : (e + some) * ROWS, :], ((0,), (0,)))
    moe = jnp.concatenate([acc[i * tokens : (i + 1) * tokens] for i in range(parts)], axis=1)
    out = (mixed_ref[...] + moe)
    first, second = out[:, : model // 2], out[:, model // 2 :]
    lower = pool_ref[0] == 0
    keep_ref[...] = jnp.where(lower, first, second).astype(BF16)
    give_ref[...] = jnp.where(lower, second, first).astype(BF16)


def combine(pool, at, gate, y, mixed):
    tokens = mixed.shape[0]
    model = mixed.shape[1]
    full = lambda a: pl.BlockSpec(a.shape, lambda i, p: (0,) * a.ndim)
    half = jax.ShapeDtypeStruct((tokens, model // 2), BF16)
    return pl.pallas_call(
        combine_kernel,
        out_shape=[half, half],
        grid_spec=pltpu.PrefetchScalarGridSpec(
            num_scalar_prefetch=1,
            grid=(1,),
            in_specs=[full(at), full(gate), full(y), pl.BlockSpec((tokens, model), lambda i, p: (0, 0))],
            out_specs=[full(half), full(half)],
        ),
        compiler_params=pltpu.CompilerParams(vmem_limit_bytes=16 * MIB),
        name="combine",
    )(pool, at, gate, y, mixed)


def body(
    queries,
    new_latent,
    cache,
    lengths,
    hidden_in,
    norm_gain,
    uv_weight,
    out_weight,
    expert_ids,
    gate_weight,
    capacity,
    gate_up,
    down,
):
    steps, demand = queries.shape[:2]
    reqs = demand // MICRO
    model = hidden_in.shape[2]
    pool = lax.axis_index("pool")
    pool_arr = jnp.full((1,), pool, jnp.int32)
    x, at, gate, mixed = attend(
        pool_arr, lengths, queries, new_latent, jnp.swapaxes(cache, 1, 2), hidden_in, norm_gain[None, :],
        uv_weight, out_weight, jnp.transpose(expert_ids, (2, 0, 1)), jnp.transpose(gate_weight, (2, 0, 1)),
        capacity[None, :],
    )
    trade = functools.partial(
        lax.all_to_all, axis_name="dev", split_axis=0, concat_axis=0, tiled=True
    )
    returned = trade(serve(trade(x), gate_up, down))
    keep, give = combine(pool_arr, at, gate, returned, mixed)
    got = lax.ppermute(give, "pool", [(0, 1), (1, 0)])
    keep = keep.reshape(steps, reqs, model // 2)
    got = got.reshape(steps, reqs, model // 2)
    return jnp.where(
        pool == 0, jnp.concatenate([keep, got], axis=1), jnp.concatenate([got, keep], axis=1)
    )


def solution(mesh):
    in_specs = (
        P(None, "dev", None, None),
        P(None, "dev", None),
        P("dev", None, None),
        P("dev"),
        P(None, "dev", None),
        P(),
        P(),
        P(),
        P(None, "dev", None),
        P(None, "dev", None),
        P(),
        P("dev", None, None),
        P("dev", None, None),
    )
    out_specs = P(None, "dev", "pool")
    return jax.shard_map(body, mesh=mesh, in_specs=in_specs, out_specs=out_specs, check_vma=False)
```

```python
import functools

import jax
import jax.numpy as jnp
from jax import lax
from jax.experimental import pallas as pl
from jax.experimental.pallas import tpu as pltpu
from jax.sharding import PartitionSpec as P

LAT = 512
ROPE = 64
QKNOPE = 128
CAP = 3
MICRO = 2
ROWS = 24
F32 = jnp.float32
BF16 = jnp.bfloat16
MIB = 1024 * 1024
ATTEND_MIB = 40
SERVE_MIB = 31


def iota(shape, dim):
    return lax.broadcasted_iota(jnp.int32, shape, dim)


def dot(a, b, contract=((1,), (0,))):
    return lax.dot_general(a, b, (contract, ((), ())), preferred_element_type=F32)


def attend_kernel(
    pool_ref, len_hbm, q_hbm, nl_hbm, cache_hbm, hid_hbm, gain_hbm, uv_hbm, ow_hbm, ids_hbm, gw_hbm, cap_hbm,
    x_ref, at_ref, gate_ref, mixed_ref,
    len_sc, q_sc, nl_sc, cache_sc, hid_sc, gain_sc, uv_sc, ow_sc, ids_sc, gw_sc, cap_sc, lat_sc, sem,
):
    pool = pool_ref[0]
    steps, reqs, heads, width = q_sc.shape
    ctx = cache_sc.shape[2]
    model = hid_sc.shape[2]
    experts = cap_sc.shape[1]
    tokens = steps * reqs
    per_req = steps * heads
    scale = (QKNOPE + ROPE) ** (-0.5)

    half = pl.ds(pool * reqs, reqs)
    moves = {}
    for i, (name, src, dst) in enumerate((
        ("len", len_hbm, len_sc),
        ("q", q_hbm.at[:, half], q_sc),
        ("nl", nl_hbm, nl_sc),
        ("cache", cache_hbm.at[half], cache_sc),
        ("ids", ids_hbm, ids_sc),
        ("gw", gw_hbm, gw_sc),
        ("cap", cap_hbm, cap_sc),
        ("uv", uv_hbm, uv_sc),
        ("hid", hid_hbm, hid_sc),
        ("gain", gain_hbm, gain_sc),
        ("ow", ow_hbm, ow_sc),
    )):
        moves[name] = pltpu.make_async_copy(src, dst, sem.at[i])
        moves[name].start()

    def mine(ref):
        wide = ref[...].astype(F32)
        part = jnp.where(pool == 0, wide[:, :reqs], wide[:, reqs:])
        return part.reshape(tokens, wide.shape[2])

    for name in ("len", "q", "nl", "ids", "gw", "cap"):
        moves[name].wait()
    demand = ids_sc.shape[2]
    cap_row = cap_sc[...].astype(F32)
    diagonal = iota((experts, experts), 0) == iota((experts, experts), 1)
    cap = jnp.sum(jnp.where(diagonal, cap_row, 0.0), axis=1, keepdims=True)
    ids = ids_sc[...]
    gates = gw_sc[...].astype(F32)
    mark = iota((experts, demand), 0)
    a, b = iota((demand, demand), 0), iota((demand, demand), 1)
    earlier = ((a // reqs == b // reqs) & (a < b)).astype(BF16)
    slots = CAP * steps
    parts = ROWS // slots
    lanes = parts * tokens
    row, lane = iota((demand, lanes), 0), iota((demand, lanes), 1)
    at = (iota((experts, lanes), 1) // tokens * slots).astype(F32)
    gate_of = jnp.zeros((experts, lanes), F32)
    for s in range(steps):
        named = jnp.zeros((experts, demand), F32)
        gate = jnp.zeros((experts, demand), F32)
        for k in range(ids.shape[0]):
            hit = ids[k, s : s + 1] == mark
            named = named + hit.astype(F32)
            gate = gate + jnp.where(hit, gates[k, s : s + 1], 0.0)
        before = dot(named.astype(BF16), earlier)
        slot = jnp.where((named > 0) & (before < cap), before + s * CAP, -100.0)
        spread = ((lane % tokens == s * reqs + row % reqs) & (row // reqs == pool)).astype(BF16)
        at = at + dot(slot.astype(BF16), spread)
        gate_of = gate_of + dot(gate.astype(BF16), spread)
    at_ref[...] = at
    gate_ref[...] = gate_of

    fresh = mine(nl_sc).astype(BF16)
    q_rows = [q_sc[:, r].astype(F32).reshape(per_req, width).astype(BF16) for r in range(reqs)]
    new = dot(jnp.concatenate(q_rows, axis=0), fresh, ((1,), (1,))) * scale
    row = iota(new.shape, 0)
    col = iota(new.shape, 1)
    valid = (row // per_req == col % reqs) & (col // reqs <= (row // heads) % steps)
    new = jnp.where(valid, new, -jnp.inf)
    moves["cache"].wait()
    position = iota((per_req, ctx), 1)
    old = []
    for r in range(reqs):
        score = dot(q_rows[r], cache_sc[r]) * scale
        old.append(jnp.where(position < len_sc[pool * reqs + r], score, -jnp.inf))
    old = jnp.concatenate(old, axis=0)
    top = jnp.maximum(jnp.max(old, axis=1, keepdims=True), jnp.max(new, axis=1, keepdims=True))
    old = jnp.exp(old - top)
    new = jnp.exp(new - top)
    total = jnp.sum(old, axis=1, keepdims=True) + jnp.sum(new, axis=1, keepdims=True)
    old = old.astype(BF16)
    latent = jnp.concatenate(
        [
            dot(old[r * per_req : (r + 1) * per_req], cache_sc[r, :LAT, :], ((1,), (1,)))
            for r in range(reqs)
        ],
        axis=0,
    )
    latent = latent + dot(new.astype(BF16), fresh[:, :LAT])
    latent = latent / total
    for i in range(lat_sc.shape[0]):
        lat_sc[i] = latent[:, i * 128 : (i + 1) * 128]
    moves["uv"].wait()
    head_out = []
    for h in range(heads):
        rows = [
            jnp.concatenate(
                [lat_sc[i, pl.ds(s * heads + h, reqs, stride=per_req), :] for i in range(lat_sc.shape[0])],
                axis=1,
            )
            for s in range(steps)
        ]
        lat_h = jnp.concatenate(rows, axis=0).astype(BF16)
        head_out.append(dot(lat_h, uv_sc[h]).astype(BF16))
    head_out = jnp.concatenate(head_out, axis=1)
    for name in ("hid", "gain", "ow"):
        moves[name].wait()
    mixed = mine(hid_sc) + dot(head_out, ow_sc[...])
    mixed_ref[...] = mixed
    normed = (
        mixed * lax.rsqrt(jnp.mean(mixed * mixed, axis=1, keepdims=True) + 1e-06) * gain_sc[...]
    ).astype(BF16)

    wide = model // parts
    stacked = jnp.concatenate([normed[:, i * wide : (i + 1) * wide] for i in range(parts)], axis=0)
    some = 16
    for e in range(0, experts, some):
        place = (iota((some, ROWS, lanes), 1).astype(F32) == at[e : e + some][:, None, :]).astype(F32)
        place = place.reshape(some * ROWS, lanes).astype(BF16)
        x_ref[e * ROWS : (e + some) * ROWS, :] = dot(place, stacked).astype(BF16)


def attend(pool, lengths, queries, new_latent, cache, hidden_in, gain, uv, ow, ids, gates, capacity):
    steps, demand, heads, width = queries.shape
    reqs = demand // MICRO
    model = hidden_in.shape[2]
    experts = capacity.shape[1]
    tokens = steps * reqs
    parts = ROWS // (CAP * steps)
    lanes = parts * tokens
    outs = [
        jax.ShapeDtypeStruct((experts * ROWS, model // parts), BF16),
        jax.ShapeDtypeStruct((experts, lanes), F32),
        jax.ShapeDtypeStruct((experts, lanes), F32),
        jax.ShapeDtypeStruct((tokens, model), F32),
    ]
    full = lambda a: pl.BlockSpec(a.shape, lambda i, p: (0,) * a.ndim)
    inputs = (lengths, queries, new_latent, cache, hidden_in, gain, uv, ow, ids, gates, capacity)
    inputs = tuple(pltpu.with_memory_space_constraint(a, pltpu.HBM) for a in inputs)
    like = lambda a: pltpu.VMEM(a.shape, a.dtype)
    return pl.pallas_call(
        attend_kernel,
        out_shape=outs,
        grid_spec=pltpu.PrefetchScalarGridSpec(
            num_scalar_prefetch=1,
            grid=(1,),
            in_specs=[pl.BlockSpec(memory_space=pltpu.HBM)] * len(inputs),
            out_specs=[full(o) for o in outs],
            scratch_shapes=[
                pltpu.SMEM(lengths.shape, lengths.dtype),
                pltpu.VMEM((steps, reqs, heads, width), BF16),
                like(new_latent),
                pltpu.VMEM((reqs,) + cache.shape[1:], BF16),
                like(hidden_in),
                like(gain),
                like(uv),
                like(ow),
                like(ids),
                like(gates),
                like(capacity),
                pltpu.VMEM((LAT // 128, tokens * heads, 128), F32),
                pltpu.SemaphoreType.DMA((len(inputs),)),
            ],
        ),
        compiler_params=pltpu.CompilerParams(vmem_limit_bytes=ATTEND_MIB * MIB),
        name="attend",
    )(pool, *inputs)


GROUP = 8


def order_matrix(slots):
    n = GROUP * ROWS
    o, i = iota((n, n), 0), iota((n, n), 1)
    per_part = GROUP * slots
    source = (o % per_part) // slots
    want = source * ROWS + (o // per_part) * slots + o % slots
    return (want == i).astype(BF16)


def serve_kernel(x_ref, gate_up_ref, down_hbm, y_ref, rows_sc, act_sc, down_sc, sem):
    model = rows_sc.shape[1]
    wide = x_ref.shape[1]
    parts = model // wide
    slots = ROWS // parts
    n = GROUP * ROWS
    per_part = GROUP * slots
    groups = x_ref.shape[0] // n
    hidden = down_hbm.shape[0]
    fetch = pltpu.make_async_copy(down_hbm, down_sc, sem)
    fetch.start()
    order = order_matrix(slots)
    for g in range(groups):
        got = dot(order, x_ref[g * n : (g + 1) * n, :]).astype(BF16)
        for i in range(parts):
            rows_sc[g * per_part : (g + 1) * per_part, i * wide : (i + 1) * wide] = got[
                i * per_part : (i + 1) * per_part
            ]
    block = 256
    for c in range(0, hidden, block):
        w = min(block, hidden - c)
        gate = dot(rows_sc[...], gate_up_ref[0, :, c : c + w])
        up = dot(rows_sc[...], gate_up_ref[0, :, hidden + c : hidden + c + w])
        act_sc[:, c : c + w] = (gate / (1.0 + jnp.exp(-gate)) * up).astype(BF16)
    fetch.wait()
    for c in range(0, model, block):
        rows_sc[:, c : c + block] = dot(act_sc[...], down_sc[:, c : c + block]).astype(BF16)
    for g in range(groups):
        piece = jnp.concatenate(
            [rows_sc[g * per_part : (g + 1) * per_part, i * wide : (i + 1) * wide] for i in range(parts)],
            axis=0,
        )
        y_ref[g * n : (g + 1) * n, :] = dot(order, piece, ((0,), (0,))).astype(BF16)


def serve(x, gate_up, down):
    n_in, wide = x.shape
    _, model, twice = gate_up.shape
    n_rows = n_in * wide // model
    vmem = pl.BlockSpec(memory_space=pltpu.VMEM)
    return pl.pallas_call(
        serve_kernel,
        out_shape=jax.ShapeDtypeStruct((n_in, wide), BF16),
        in_specs=[vmem, vmem, pl.BlockSpec(memory_space=pl.ANY)],
        out_specs=vmem,
        scratch_shapes=[
            pltpu.VMEM((n_rows, model), BF16),
            pltpu.VMEM((n_rows, twice // 2), BF16),
            pltpu.VMEM(down.shape[1:], BF16),
            pltpu.SemaphoreType.DMA,
        ],
        compiler_params=pltpu.CompilerParams(vmem_limit_bytes=SERVE_MIB * MIB),
        name="serve",
    )(x, gate_up, pltpu.with_memory_space_constraint(down[0], pltpu.HBM))


def combine_kernel(pool_ref, at_ref, gate_ref, y_ref, mixed_ref, keep_ref, give_ref):
    experts, lanes = at_ref.shape
    tokens, model = mixed_ref.shape
    parts = lanes // tokens
    wide = model // parts
    some = 16
    acc = jnp.zeros((lanes, wide), F32)
    for e in range(0, experts, some):
        hit = iota((some, ROWS, lanes), 1).astype(F32) == at_ref[e : e + some][:, None, :]
        weight = jnp.where(hit, gate_ref[e : e + some][:, None, :], 0.0)
        weight = weight.reshape(some * ROWS, lanes).astype(BF16)
        acc = acc + dot(weight, y_ref[e * ROWS : (e + some) * ROWS, :], ((0,), (0,)))
    moe = jnp.concatenate([acc[i * tokens : (i + 1) * tokens] for i in range(parts)], axis=1)
    out = (mixed_ref[...] + moe)
    first, second = out[:, : model // 2], out[:, model // 2 :]
    lower = pool_ref[0] == 0
    keep_ref[...] = jnp.where(lower, first, second).astype(BF16)
    give_ref[...] = jnp.where(lower, second, first).astype(BF16)


def combine(pool, at, gate, y, mixed):
    tokens = mixed.shape[0]
    model = mixed.shape[1]
    full = lambda a: pl.BlockSpec(a.shape, lambda i, p: (0,) * a.ndim)
    half = jax.ShapeDtypeStruct((tokens, model // 2), BF16)
    return pl.pallas_call(
        combine_kernel,
        out_shape=[half, half],
        grid_spec=pltpu.PrefetchScalarGridSpec(
            num_scalar_prefetch=1,
            grid=(1,),
            in_specs=[full(at), full(gate), full(y), pl.BlockSpec((tokens, model), lambda i, p: (0, 0))],
            out_specs=[full(half), full(half)],
        ),
        compiler_params=pltpu.CompilerParams(vmem_limit_bytes=16 * MIB),
        name="combine",
    )(pool, at, gate, y, mixed)


def body(
    queries,
    new_latent,
    cache,
    lengths,
    hidden_in,
    norm_gain,
    uv_weight,
    out_weight,
    expert_ids,
    gate_weight,
    capacity,
    gate_up,
    down,
):
    steps, demand = queries.shape[:2]
    reqs = demand // MICRO
    model = hidden_in.shape[2]
    pool = lax.axis_index("pool")
    pool_arr = jnp.full((1,), pool, jnp.int32)
    x, at, gate, mixed = attend(
        pool_arr, lengths, queries, new_latent, jnp.swapaxes(cache, 1, 2), hidden_in, norm_gain[None, :],
        uv_weight, out_weight, jnp.transpose(expert_ids, (2, 0, 1)), jnp.transpose(gate_weight, (2, 0, 1)),
        capacity[None, :],
    )
    trade = functools.partial(
        lax.all_to_all, axis_name="dev", split_axis=0, concat_axis=0, tiled=True
    )
    returned = trade(serve(trade(x), gate_up, down))
    keep, give = combine(pool_arr, at, gate, returned, mixed)
    got = lax.ppermute(give, "pool", [(0, 1), (1, 0)])
    keep = keep.reshape(steps, reqs, model // 2)
    got = got.reshape(steps, reqs, model // 2)
    return jnp.where(
        pool == 0, jnp.concatenate([keep, got], axis=1), jnp.concatenate([got, keep], axis=1)
    )


def solution(mesh):
    in_specs = (
        P(None, "dev", None, None),
        P(None, "dev", None),
        P("dev", None, None),
        P("dev"),
        P(None, "dev", None),
        P(),
        P(),
        P(),
        P(None, "dev", None),
        P(None, "dev", None),
        P(),
        P("dev", None, None),
        P("dev", None, None),
    )
    out_specs = P(None, "dev", "pool")
    return jax.shard_map(body, mesh=mesh, in_specs=in_specs, out_specs=out_specs, check_vma=False)
```

```python
import functools

import jax
import jax.numpy as jnp
from jax import lax
from jax.experimental import pallas as pl
from jax.experimental.pallas import tpu as pltpu
from jax.sharding import PartitionSpec as P

LAT = 512
ROPE = 64
QKNOPE = 128
CAP = 3
MICRO = 2
ROWS = 24
F32 = jnp.float32
BF16 = jnp.bfloat16
MIB = 1024 * 1024
ATTEND_MIB = 40
SERVE_MIB = 31


def iota(shape, dim):
    return lax.broadcasted_iota(jnp.int32, shape, dim)


def dot(a, b, contract=((1,), (0,))):
    return lax.dot_general(a, b, (contract, ((), ())), preferred_element_type=F32)


def attend_kernel(
    pool_ref, len_hbm, q_hbm, nl_hbm, cache_hbm, hid_hbm, gain_hbm, uv_hbm, ow_hbm, ids_hbm, gw_hbm, cap_hbm,
    x_ref, at_ref, gate_ref, mixed_ref,
    len_sc, q_sc, nl_sc, cache_sc, hid_sc, gain_sc, uv_sc, ow_sc, ids_sc, gw_sc, cap_sc, lat_sc, sem,
):
    pool = pool_ref[0]
    steps, reqs, heads, width = q_sc.shape
    ctx = cache_sc.shape[2]
    model = hid_sc.shape[2]
    experts = cap_sc.shape[1]
    tokens = steps * reqs
    per_req = steps * heads
    scale = (QKNOPE + ROPE) ** (-0.5)

    half = pl.ds(pool * reqs, reqs)
    moves = {}
    for i, (name, src, dst) in enumerate((
        ("len", len_hbm, len_sc),
        ("q", q_hbm.at[:, half], q_sc),
        ("nl", nl_hbm, nl_sc),
        ("cache", cache_hbm.at[half], cache_sc),
        ("ids", ids_hbm, ids_sc),
        ("gw", gw_hbm, gw_sc),
        ("cap", cap_hbm, cap_sc),
        ("uv", uv_hbm, uv_sc),
        ("hid", hid_hbm, hid_sc),
        ("gain", gain_hbm, gain_sc),
        ("ow", ow_hbm, ow_sc),
    )):
        moves[name] = pltpu.make_async_copy(src, dst, sem.at[i])
        moves[name].start()

    def mine(ref):
        wide = ref[...].astype(F32)
        part = jnp.where(pool == 0, wide[:, :reqs], wide[:, reqs:])
        return part.reshape(tokens, wide.shape[2])

    for name in ("len", "q", "nl", "ids", "gw", "cap"):
        moves[name].wait()
    demand = ids_sc.shape[2]
    cap_row = cap_sc[...].astype(F32)
    diagonal = iota((experts, experts), 0) == iota((experts, experts), 1)
    cap = jnp.sum(jnp.where(diagonal, cap_row, 0.0), axis=1, keepdims=True)
    ids = ids_sc[...]
    gates = gw_sc[...].astype(F32)
    mark = iota((experts, demand), 0)
    a, b = iota((demand, demand), 0), iota((demand, demand), 1)
    earlier = ((a // reqs == b // reqs) & (a < b)).astype(BF16)
    slots = CAP * steps
    parts = ROWS // slots
    lanes = parts * tokens
    row, lane = iota((demand, lanes), 0), iota((demand, lanes), 1)
    at = (iota((experts, lanes), 1) // tokens * slots).astype(F32)
    gate_of = jnp.zeros((experts, lanes), F32)
    for s in range(steps):
        named = jnp.zeros((experts, demand), F32)
        gate = jnp.zeros((experts, demand), F32)
        for k in range(ids.shape[0]):
            hit = ids[k, s : s + 1] == mark
            named = named + hit.astype(F32)
            gate = gate + jnp.where(hit, gates[k, s : s + 1], 0.0)
        before = dot(named.astype(BF16), earlier)
        slot = jnp.where((named > 0) & (before < cap), before + s * CAP, -100.0)
        spread = ((lane % tokens == s * reqs + row % reqs) & (row // reqs == pool)).astype(BF16)
        at = at + dot(slot.astype(BF16), spread)
        gate_of = gate_of + dot(gate.astype(BF16), spread)
    at_ref[...] = at
    gate_ref[...] = gate_of

    fresh = mine(nl_sc).astype(BF16)
    q_rows = [q_sc[:, r].astype(F32).reshape(per_req, width).astype(BF16) for r in range(reqs)]
    new = dot(jnp.concatenate(q_rows, axis=0), fresh, ((1,), (1,))) * scale
    row = iota(new.shape, 0)
    col = iota(new.shape, 1)
    valid = (row // per_req == col % reqs) & (col // reqs <= (row // heads) % steps)
    new = jnp.where(valid, new, -jnp.inf)
    moves["cache"].wait()
    position = iota((per_req, ctx), 1)
    old = []
    for r in range(reqs):
        score = dot(q_rows[r], cache_sc[r]) * scale
        old.append(jnp.where(position < len_sc[pool * reqs + r], score, -jnp.inf))
    old = jnp.concatenate(old, axis=0)
    top = jnp.maximum(jnp.max(old, axis=1, keepdims=True), jnp.max(new, axis=1, keepdims=True))
    old = jnp.exp(old - top)
    new = jnp.exp(new - top)
    total = jnp.sum(old, axis=1, keepdims=True) + jnp.sum(new, axis=1, keepdims=True)
    old = old.astype(BF16)
    latent = jnp.concatenate(
        [
            dot(old[r * per_req : (r + 1) * per_req], cache_sc[r, :LAT, :], ((1,), (1,)))
            for r in range(reqs)
        ],
        axis=0,
    )
    latent = latent + dot(new.astype(BF16), fresh[:, :LAT])
    latent = latent / total
    for i in range(lat_sc.shape[0]):
        lat_sc[i] = latent[:, i * 128 : (i + 1) * 128]
    moves["uv"].wait()
    head_out = []
    for h in range(heads):
        rows = [
            jnp.concatenate(
                [lat_sc[i, pl.ds(s * heads + h, reqs, stride=per_req), :] for i in range(lat_sc.shape[0])],
                axis=1,
            )
            for s in range(steps)
        ]
        lat_h = jnp.concatenate(rows, axis=0).astype(BF16)
        head_out.append(dot(lat_h, uv_sc[h]).astype(BF16))
    head_out = jnp.concatenate(head_out, axis=1)
    for name in ("hid", "gain", "ow"):
        moves[name].wait()
    mixed = mine(hid_sc) + dot(head_out, ow_sc[...])
    mixed_ref[...] = mixed
    normed = (
        mixed * lax.rsqrt(jnp.mean(mixed * mixed, axis=1, keepdims=True) + 1e-06) * gain_sc[...]
    ).astype(BF16)

    wide = model // parts
    stacked = jnp.concatenate([normed[:, i * wide : (i + 1) * wide] for i in range(parts)], axis=0)
    some = 16
    for e in range(0, experts, some):
        place = (iota((some, ROWS, lanes), 1).astype(F32) == at[e : e + some][:, None, :]).astype(F32)
        place = place.reshape(some * ROWS, lanes).astype(BF16)
        x_ref[e * ROWS : (e + some) * ROWS, :] = dot(place, stacked).astype(BF16)


def attend(pool, lengths, queries, new_latent, cache, hidden_in, gain, uv, ow, ids, gates, capacity):
    steps, demand, heads, width = queries.shape
    reqs = demand // MICRO
    model = hidden_in.shape[2]
    experts = capacity.shape[1]
    tokens = steps * reqs
    parts = ROWS // (CAP * steps)
    lanes = parts * tokens
    outs = [
        jax.ShapeDtypeStruct((experts * ROWS, model // parts), BF16),
        jax.ShapeDtypeStruct((experts, lanes), F32),
        jax.ShapeDtypeStruct((experts, lanes), F32),
        jax.ShapeDtypeStruct((tokens, model), F32),
    ]
    inputs = (lengths, queries, new_latent, cache, hidden_in, gain, uv, ow, ids, gates, capacity)
    inputs = tuple(pltpu.with_memory_space_constraint(a, pltpu.HBM) for a in inputs)
    like = lambda a: pltpu.VMEM(a.shape, a.dtype)
    return pl.pallas_call(
        attend_kernel,
        out_shape=outs,
        in_specs=[pl.BlockSpec(memory_space=pltpu.SMEM)] + [pl.BlockSpec(memory_space=pltpu.HBM)] * len(inputs),
        out_specs=[pl.BlockSpec(memory_space=pltpu.VMEM)] * len(outs),
        scratch_shapes=[
            pltpu.SMEM(lengths.shape, lengths.dtype),
            pltpu.VMEM((steps, reqs, heads, width), BF16),
            like(new_latent),
            pltpu.VMEM((reqs,) + cache.shape[1:], BF16),
            like(hidden_in),
            like(gain),
            like(uv),
            like(ow),
            like(ids),
            like(gates),
            like(capacity),
            pltpu.VMEM((LAT // 128, tokens * heads, 128), F32),
            pltpu.SemaphoreType.DMA((len(inputs),)),
        ],
        compiler_params=pltpu.CompilerParams(vmem_limit_bytes=ATTEND_MIB * MIB),
        name="attend",
    )(pool, *inputs)


GROUP = 8


def order_matrix(slots):
    n = GROUP * ROWS
    o, i = iota((n, n), 0), iota((n, n), 1)
    per_part = GROUP * slots
    source = (o % per_part) // slots
    want = source * ROWS + (o // per_part) * slots + o % slots
    return (want == i).astype(BF16)


def serve_kernel(x_ref, gate_up_ref, down_hbm, y_ref, rows_sc, act_sc, down_sc, sem):
    model = rows_sc.shape[1]
    wide = x_ref.shape[1]
    parts = model // wide
    slots = ROWS // parts
    n = GROUP * ROWS
    per_part = GROUP * slots
    groups = x_ref.shape[0] // n
    hidden = down_hbm.shape[0]
    fetch = pltpu.make_async_copy(down_hbm, down_sc, sem)
    fetch.start()
    order = order_matrix(slots)
    for g in range(groups):
        got = dot(order, x_ref[g * n : (g + 1) * n, :]).astype(BF16)
        for i in range(parts):
            rows_sc[g * per_part : (g + 1) * per_part, i * wide : (i + 1) * wide] = got[
                i * per_part : (i + 1) * per_part
            ]
    block = 256
    for c in range(0, hidden, block):
        w = min(block, hidden - c)
        gate = dot(rows_sc[...], gate_up_ref[0, :, c : c + w])
        up = dot(rows_sc[...], gate_up_ref[0, :, hidden + c : hidden + c + w])
        act_sc[:, c : c + w] = (gate / (1.0 + jnp.exp(-gate)) * up).astype(BF16)
    fetch.wait()
    for c in range(0, model, block):
        rows_sc[:, c : c + block] = dot(act_sc[...], down_sc[:, c : c + block]).astype(BF16)
    for g in range(groups):
        piece = jnp.concatenate(
            [rows_sc[g * per_part : (g + 1) * per_part, i * wide : (i + 1) * wide] for i in range(parts)],
            axis=0,
        )
        y_ref[g * n : (g + 1) * n, :] = dot(order, piece, ((0,), (0,))).astype(BF16)


def serve(x, gate_up, down):
    n_in, wide = x.shape
    _, model, twice = gate_up.shape
    n_rows = n_in * wide // model
    vmem = pl.BlockSpec(memory_space=pltpu.VMEM)
    return pl.pallas_call(
        serve_kernel,
        out_shape=jax.ShapeDtypeStruct((n_in, wide), BF16),
        in_specs=[vmem, vmem, pl.BlockSpec(memory_space=pl.ANY)],
        out_specs=vmem,
        scratch_shapes=[
            pltpu.VMEM((n_rows, model), BF16),
            pltpu.VMEM((n_rows, twice // 2), BF16),
            pltpu.VMEM(down.shape[1:], BF16),
            pltpu.SemaphoreType.DMA,
        ],
        compiler_params=pltpu.CompilerParams(vmem_limit_bytes=SERVE_MIB * MIB),
        name="serve",
    )(x, gate_up, pltpu.with_memory_space_constraint(down[0], pltpu.HBM))


def combine_kernel(pool_ref, at_ref, gate_ref, y_ref, mixed_ref, keep_ref, give_ref):
    experts, lanes = at_ref.shape
    tokens, model = mixed_ref.shape
    parts = lanes // tokens
    wide = model // parts
    some = 16
    acc = jnp.zeros((lanes, wide), F32)
    for e in range(0, experts, some):
        hit = iota((some, ROWS, lanes), 1).astype(F32) == at_ref[e : e + some][:, None, :]
        weight = jnp.where(hit, gate_ref[e : e + some][:, None, :], 0.0)
        weight = weight.reshape(some * ROWS, lanes).astype(BF16)
        acc = acc + dot(weight, y_ref[e * ROWS : (e + some) * ROWS, :], ((0,), (0,)))
    moe = jnp.concatenate([acc[i * tokens : (i + 1) * tokens] for i in range(parts)], axis=1)
    out = (mixed_ref[...] + moe)
    first, second = out[:, : model // 2], out[:, model // 2 :]
    lower = pool_ref[0] == 0
    keep_ref[...] = jnp.where(lower, first, second).astype(BF16)
    give_ref[...] = jnp.where(lower, second, first).astype(BF16)


def combine(pool, at, gate, y, mixed):
    tokens = mixed.shape[0]
    model = mixed.shape[1]
    full = lambda a: pl.BlockSpec(a.shape, lambda i, p: (0,) * a.ndim)
    half = jax.ShapeDtypeStruct((tokens, model // 2), BF16)
    return pl.pallas_call(
        combine_kernel,
        out_shape=[half, half],
        grid_spec=pltpu.PrefetchScalarGridSpec(
            num_scalar_prefetch=1,
            grid=(1,),
            in_specs=[full(at), full(gate), full(y), pl.BlockSpec((tokens, model), lambda i, p: (0, 0))],
            out_specs=[full(half), full(half)],
        ),
        compiler_params=pltpu.CompilerParams(vmem_limit_bytes=16 * MIB),
        name="combine",
    )(pool, at, gate, y, mixed)


def body(
    queries,
    new_latent,
    cache,
    lengths,
    hidden_in,
    norm_gain,
    uv_weight,
    out_weight,
    expert_ids,
    gate_weight,
    capacity,
    gate_up,
    down,
):
    steps, demand = queries.shape[:2]
    reqs = demand // MICRO
    model = hidden_in.shape[2]
    pool = lax.axis_index("pool")
    pool_arr = jnp.full((1,), pool, jnp.int32)
    x, at, gate, mixed = attend(
        pool_arr, lengths, queries, new_latent, jnp.swapaxes(cache, 1, 2), hidden_in, norm_gain[None, :],
        uv_weight, out_weight, jnp.transpose(expert_ids, (2, 0, 1)), jnp.transpose(gate_weight, (2, 0, 1)),
        capacity[None, :],
    )
    trade = functools.partial(
        lax.all_to_all, axis_name="dev", split_axis=0, concat_axis=0, tiled=True
    )
    returned = trade(serve(trade(x), gate_up, down))
    keep, give = combine(pool_arr, at, gate, returned, mixed)
    got = lax.ppermute(give, "pool", [(0, 1), (1, 0)])
    keep = keep.reshape(steps, reqs, model // 2)
    got = got.reshape(steps, reqs, model // 2)
    return jnp.where(
        pool == 0, jnp.concatenate([keep, got], axis=1), jnp.concatenate([got, keep], axis=1)
    )


def solution(mesh):
    in_specs = (
        P(None, "dev", None, None),
        P(None, "dev", None),
        P("dev", None, None),
        P("dev"),
        P(None, "dev", None),
        P(),
        P(),
        P(),
        P(None, "dev", None),
        P(None, "dev", None),
        P(),
        P("dev", None, None),
        P("dev", None, None),
    )
    out_specs = P(None, "dev", "pool")
    return jax.shard_map(body, mesh=mesh, in_specs=in_specs, out_specs=out_specs, check_vma=False)
```
